256 devices in a mesh: ctx: 16 (over y_hi, x, core), head: 16 (over y_lo, z).
Axes of the slice: x: 4, y: 4 (y_hi: 2, y_lo: 2; y = y_hi * 2 + y_lo), z: 8, core: 2. Of those that a mesh axis runs over, the one named last changes fastest.
Arguments:
- query_latent: bfloat16 [4096, 1536], P(('ctx', 'head')), may hold values from -6 to 6
- norm_gain: bfloat16 [1536], replicated, may hold values from 0.099609375 to 1.8984375
- kv_latent: bfloat16 [4096, 576], P(('ctx', 'head')), may hold values from -120 to 120
- q_up: bfloat16 [1536, 12288], P(None, 'head'), may hold values from -0.15625 to 0.15625
- absorb_key: bfloat16 [64, 128, 512], P('head'), may hold values from -0.5 to 0.5
- absorb_value: bfloat16 [64, 512, 128], P('head'), may hold values from -0.25 to 0.25
- block_owner: int32 [16], replicated, may hold values from 0 to 15, each once
Outputs:
- head_output: bfloat16 [4096, 8192], P('ctx', 'head')
The draws below stay inside these ranges and needn't reach their ends.
All inputs are finite; a program needn't handle non-finite values.
Results may differ from the reference program's by a relative error of at most 0.024.
The reference program's roundings to bfloat16 on the way (of `normed`, `q_nope`, `q_pe`, `q_abs`, `weights` and `latent_out`) count: a program that leaves them out, or rounds other values in their place, can miss the bound.
Values may be sent and summed in bfloat16 or wider, within the bound.
No kernel may reach another device: no remote copies, remote signals or barrier semaphores. Data moves between devices by JAX's collectives and lax.ppermute only.
A program may use at most 64 MiB of HBM per device.

```python
import math
import jax
import jax.numpy as jnp
from jax import lax

QLAT = 1536
LATENT = 512
ROPE = 64
NOPE = 128
VHEAD = 128
TOK_DEV = 256
HEADS = 64
TOKENS = 4096
N_CTX = 16


def draw_kv_latent(key, part):
    row_count = TOKENS
    kv_width = LATENT + ROPE
    first_key = jax.random.fold_in(jax.random.fold_in(key, 17), 0)
    values = jax.random.normal(first_key, (row_count, kv_width), jnp.float32)
    return jnp.clip(values, -6.0, 6.0).astype(jnp.bfloat16)


def block_levels(key, shape, cuts, least, top_value):
    gain = 1.0
    for dim, parts in cuts:
        draws = jax.random.uniform(jax.random.fold_in(jax.random.fold_in(key, 6), dim), (parts,), jnp.float32, least / len(cuts), top_value / len(cuts))
        gain = gain * jnp.repeat(jnp.exp(draws), shape[dim] // parts).reshape((-1,) + (1,) * (len(shape) - 1 - dim))
    return gain


def normal_values(own_key, extent, spread, limit, pieces=(), held_as=jnp.bfloat16):
    entries = jax.random.normal(own_key, extent, jnp.float32) * spread
    if len(pieces) > 0:
        entries = block_levels(own_key, extent, pieces, -0.22, 0.18) * entries
    return jnp.clip(entries, min=-limit, max=limit).astype(held_as)


def setup_inputs(seed: int = 0) -> dict:
    key_list = jax.random.split(jax.random.key(seed), 8)
    return {
        "query_latent": normal_values(key_list[0], (TOKENS, QLAT), 1.0, 6.0, ((0, 256),)),
        "norm_gain": jnp.clip(1.0 + 0.18 * jax.random.normal(key_list[1], (QLAT,), jnp.float32), 0.099609375, 1.8984375).astype(jnp.bfloat16),
        "kv_latent": draw_kv_latent(jax.random.fold_in(key_list[7], 71), 0),
        "q_up": normal_values(key_list[3], (QLAT, HEADS * (NOPE + ROPE)), QLAT ** -0.5, 0.15625, ((1, 16),)),
        "absorb_key": normal_values(key_list[4], (HEADS, NOPE, LATENT), NOPE ** -0.5, 0.5, ((0, 16),)),
        "absorb_value": normal_values(key_list[5], (HEADS, LATENT, VHEAD), LATENT ** -0.5, 0.25, ((0, 16),)),
        "block_owner": jax.random.permutation(key_list[6], N_CTX).astype(jnp.int32),
    }


epsilon = 1e-06
masked_score = -1e+30

def row_positions(block_owner):
    row_ids = jnp.arange(TOKENS, dtype=jnp.int32)
    device = row_ids // TOK_DEV
    offset = row_ids % TOK_DEV
    half_len = TOK_DEV // 2
    ctx_ids = jnp.arange(N_CTX, dtype=jnp.int32)
    owner_ctx = lax.optimization_barrier(jnp.sum(jnp.where(device[:, None] == ctx_ids[None, :], block_owner[None, :], 0), axis=1))
    half_block = jnp.where(offset // half_len == 0, owner_ctx, 2 * N_CTX - 1 - owner_ctx)
    return (half_block * half_len + offset % half_len).astype(jnp.int32)

def rotate(values, positions):
    half_width = values.shape[-1] // 2
    frequency = jnp.exp(jnp.arange(half_width, dtype=jnp.float32) * (-math.log(10000.0) / half_width))
    angles = positions.astype(jnp.float32)[:, None, None] * frequency
    cosine = jnp.cos(angles)
    sine = jnp.sin(angles)
    front = values[..., :half_width]
    back = values[..., half_width:]
    return jnp.concatenate([front * cosine - back * sine, front * sine + back * cosine], axis=-1)

def reference(query_latent, norm_gain, kv_latent, q_up, absorb_key, absorb_value, block_owner):
    positions = row_positions(block_owner)
    query_f32 = query_latent.astype(jnp.float32)
    normed = (query_f32 * lax.rsqrt(lax.optimization_barrier(jnp.mean(query_f32 * query_f32, axis=-1, keepdims=True)) + epsilon) * norm_gain.astype(jnp.float32)).astype(jnp.bfloat16)
    projected = jnp.dot(normed, q_up, preferred_element_type=jnp.float32).reshape(TOKENS, HEADS, NOPE + ROPE)
    q_nope = projected[..., :NOPE].astype(jnp.bfloat16)
    q_pe = rotate(projected[..., NOPE:], positions).astype(jnp.bfloat16)
    q_abs = jnp.einsum('thn,hnc->thc', q_nope.astype(jnp.float32), absorb_key.astype(jnp.float32)).astype(jnp.bfloat16)
    queries = jnp.concatenate([q_abs, q_pe], axis=-1)
    blocks = queries.reshape(N_CTX, TOK_DEV, HEADS, LATENT + ROPE).transpose(0, 2, 1, 3)
    blocks = blocks.reshape(N_CTX * HEADS, TOK_DEV, LATENT + ROPE)
    block_positions = positions.reshape(N_CTX, TOK_DEV)
    score_scale = float(NOPE + ROPE) ** (-0.5)
    latent_values = kv_latent[:, :LATENT]

    def attend(flat_index):
        block_id = flat_index // HEADS
        query_rows = lax.dynamic_index_in_dim(blocks, flat_index, 0, keepdims=False)
        query_positions = lax.dynamic_index_in_dim(block_positions, block_id, 0, keepdims=False)
        scores = jnp.dot(query_rows, kv_latent.T, preferred_element_type=jnp.float32) * score_scale
        allowed = positions[None, :] <= query_positions[:, None]
        scores = jnp.where(allowed, scores, masked_score)
        row_peak = lax.optimization_barrier(jnp.max(scores, axis=-1, keepdims=True))
        weights = jnp.where(allowed, jnp.exp(scores - row_peak), 0.0)
        row_total = lax.optimization_barrier(jnp.sum(weights, axis=-1, keepdims=True))
        summed = jnp.dot(weights.astype(jnp.bfloat16), latent_values, preferred_element_type=jnp.float32)
        return (summed / row_total).astype(jnp.bfloat16)
    latent_out = lax.map(attend, jnp.arange(N_CTX * HEADS, dtype=jnp.int32))
    latent_out = latent_out.reshape(N_CTX, HEADS, TOK_DEV, LATENT).transpose(0, 2, 1, 3).reshape(TOKENS, HEADS, LATENT)
    head_output = jnp.einsum('thc,hcv->thv', latent_out.astype(jnp.float32), absorb_value.astype(jnp.float32))
    return head_output.astype(jnp.bfloat16).reshape(TOKENS, HEADS * VHEAD)
```

```python
import math

import jax
import jax.numpy as jnp
from jax import lax
from jax.experimental import pallas as pl
from jax.experimental.pallas import tpu as pltpu
from jax.sharding import PartitionSpec as P

QLAT = 1536
LATENT = 512
ROPE = 64
NOPE = 128
KV = LATENT + ROPE
HD = 4
HALF = 128
NB = 32
EPS = 1e-06
SCALE2 = float(NOPE + ROPE) ** (-0.5) * math.log2(math.e)
MASKED = -1e30
AXES = ("ctx", "head")
SHIFTS = (1, 3, 2)


def flat(x, y, z, c):
    x, y, z, c = x % 4, y % 4, z % 8, c % 2
    return (((y // 2) * 4 + x) * 2 + c) * 16 + (y % 2) * 8 + z


def move(a, to):
    pairs = []
    for x in range(4):
        for y in range(4):
            for z in range(8):
                for c in range(2):
                    pairs.append((flat(x, y, z, c), flat(*to(x, y, z, c))))
    return lax.ppermute(a, AXES, pairs)


def shift(k, first):
    def to(x, y, z, c):
        return (x + k, y, z, c) if (c == 0) == first else (x, y + k, z, c)

    return to


def swap_core(x, y, z, c):
    return (x, y, z, c + 1)


def project_kernel(q_ref, gain_ref, cos_ref, sin_ref, up_ref, ak_ref, out_ref):
    x = q_ref[...].astype(jnp.float32)
    ms = jnp.mean(x * x, axis=-1, keepdims=True)
    normed = (x * lax.rsqrt(ms + EPS) * gain_ref[...].astype(jnp.float32)).astype(jnp.bfloat16)
    proj = jnp.dot(normed, up_ref[...], preferred_element_type=jnp.float32)
    cos, sin = cos_ref[...], sin_ref[...]
    for h in range(HD):
        base = h * (NOPE + ROPE)
        nope = proj[:, base : base + NOPE].astype(jnp.bfloat16)
        a = proj[:, base + NOPE : base + NOPE + ROPE // 2]
        b = proj[:, base + NOPE + ROPE // 2 : base + NOPE + ROPE]
        pe = jnp.concatenate([a * cos - b * sin, a * sin + b * cos], axis=-1).astype(jnp.bfloat16)
        qa = jnp.dot(nope, ak_ref[h], preferred_element_type=jnp.float32).astype(jnp.bfloat16)
        for half in range(2):
            r = (half * HD + h) * HALF
            out_ref[r : r + HALF, :LATENT] = qa[half * HALF : (half + 1) * HALF]
            out_ref[r : r + HALF, LATENT:] = pe[half * HALF : (half + 1) * HALF]


def attend_kernel(place_ref, owner_ref, q_ref, av_ref, *rest):
    pieces = rest[:8]
    out_ref = rest[8]
    kv, acc, m_ref, l_ref, sems = rest[9:]
    me_x, me_y, me_c = place_ref[0], place_ref[1], place_ref[2]

    def copy(src, b):
        return pltpu.make_async_copy(
            src, kv.at[pl.ds(pl.multiple_of(b * HALF, HALF), HALF)], sems.at[b]
        )

    offs = (0,) + SHIFTS
    for far in range(2):
        core = me_c if far == 0 else 1 - me_c
        for j in range(4):
            for i in range(4):
                first, second = offs[i], offs[j]
                dx = jnp.where(core == 0, first, second)
                dy = jnp.where(core == 0, second, first)
                x = (me_x - dx + 4) % 4
                y = (me_y - dy + 4) % 4
                p = owner_ref[((y // 2) * 4 + x) * 2 + core]
                b = jnp.where(y % 2 == 0, p, NB - 1 - p)
                copy(pieces[far * 4 + j].at[i * HALF : (i + 1) * HALF], b).start()

    mine = owner_ref[((me_y // 2) * 4 + me_x) * 2 + me_c]

    def wait(b):
        copy(pieces[0].at[0:HALF], b).wait()

    def tile(half, j, masked, a):
        keys = kv[pl.ds(pl.multiple_of(j * 256, 256), 256), :]
        vals = keys[:, :LATENT]
        for g in range(4):
            r = half * 512 + g * HALF
            s = lax.dot_general(
                q_ref[r : r + HALF, :], keys, (((1,), (1,)), ((), ())),
                preferred_element_type=jnp.float32,
            )
            if masked:
                col = lax.broadcasted_iota(jnp.int32, (HALF, 256), 1) + j * 256
                row = lax.broadcasted_iota(jnp.int32, (HALF, 256), 0) + a * HALF
                s = jnp.where(col <= row, s, MASKED)
            rows = slice(g * HALF, (g + 1) * HALF)
            old = m_ref[rows]
            new = jnp.maximum(old, jnp.max(s, axis=-1, keepdims=True))
            w = jnp.exp2((s - new[:, :1]) * SCALE2)
            f = jnp.exp2((old - new) * SCALE2)
            m_ref[rows] = new
            l_ref[rows] = l_ref[rows] * f + (w[:, :128] + w[:, 128:])
            acc[rows] = acc[rows] * f[:, :1] + jnp.dot(
                w.astype(jnp.bfloat16), vals, preferred_element_type=jnp.float32
            )

    seen = 0
    for half in range(2):
        a = mine if half == 0 else NB - 1 - mine
        m_ref[...] = jnp.full_like(m_ref, MASKED)
        l_ref[...] = jnp.zeros_like(l_ref)
        acc[...] = jnp.zeros_like(acc)
        last = a // 2

        def step(j, _):
            @pl.when(j >= seen)
            def _():
                wait(2 * j)
                wait(2 * j + 1)

            tile(half, j, False, a)
            return 0

        lax.fori_loop(0, last, step, 0)

        @pl.when(last >= seen)
        def _():
            wait(2 * last)
            wait(2 * last + 1)

        tile(half, last, True, a)
        seen = last + 1
        for g in range(HD):
            rows = slice(g * HALF, (g + 1) * HALF)
            total = jnp.sum(l_ref[rows], axis=-1, keepdims=True)
            lat = (acc[rows] / total).astype(jnp.bfloat16)
            out_ref[half * HALF : (half + 1) * HALF, g * HALF : (g + 1) * HALF] = jnp.dot(
                lat, av_ref[g], preferred_element_type=jnp.float32
            ).astype(jnp.bfloat16)

    def drain(j, _):
        wait(2 * j)
        wait(2 * j + 1)
        return 0

    lax.fori_loop(seen, NB // 2, drain, 0)


def per_device(query_latent, norm_gain, kv_latent, q_up, absorb_key, absorb_value, block_owner):
    ctx, head = lax.axis_index("ctx"), lax.axis_index("head")
    me_x, me_y, me_c = (ctx // 2) % 4, (ctx // 8) * 2 + head // 8, ctx % 2
    place = jnp.stack([me_x, me_y, me_c]).astype(jnp.int32)

    z_groups = [list(range(8)), list(range(8, 16))]
    own = lax.all_to_all(
        jnp.broadcast_to(kv_latent[None], (8,) + kv_latent.shape),
        "head", 0, 0, axis_index_groups=z_groups, tiled=True,
    ).reshape(HALF, KV)
    ring = jnp.concatenate([own] + [move(own, shift(k, True)) for k in SHIFTS], axis=0)
    mine = [ring] + [move(ring, shift(k, False)) for k in SHIFTS]
    other = [move(t, swap_core) for t in mine]

    rows = lax.all_to_all(
        jnp.broadcast_to(query_latent[None], (16,) + query_latent.shape),
        "head", 0, 0, tiled=True,
    ).reshape(256, QLAT)
    p = block_owner[ctx]
    offset = jnp.arange(256, dtype=jnp.int32)
    pos = jnp.where(offset < HALF, p * HALF + offset, (NB - 1 - p) * HALF + offset - HALF)
    freq = jnp.exp(jnp.arange(ROPE // 2, dtype=jnp.float32) * (-math.log(10000.0) / (ROPE // 2)))
    angles = pos.astype(jnp.float32)[:, None] * freq
    vm = pl.BlockSpec(memory_space=pltpu.VMEM)
    queries = pl.pallas_call(
        project_kernel,
        out_shape=jax.ShapeDtypeStruct((1024, KV), jnp.bfloat16),
        in_specs=[vm] * 6,
        out_specs=vm,
        compiler_params=pltpu.CompilerParams(vmem_limit_bytes=24 * 2**20),
        cost_estimate=pl.CostEstimate(flops=750_000_000, bytes_accessed=5_000_000, transcendentals=0),
    )(rows, norm_gain.reshape(1, QLAT), jnp.cos(angles), jnp.sin(angles), q_up, absorb_key)

    sm = pl.BlockSpec(memory_space=pltpu.SMEM)
    return pl.pallas_call(
        attend_kernel,
        out_shape=jax.ShapeDtypeStruct((256, 512), jnp.bfloat16),
        in_specs=[sm, sm, vm, vm] + [pl.BlockSpec(memory_space=pl.ANY)] * 8,
        out_specs=vm,
        scratch_shapes=[
            pltpu.VMEM((NB * HALF, KV), jnp.bfloat16),
            pltpu.VMEM((512, LATENT), jnp.float32),
            pltpu.VMEM((512, 128), jnp.float32),
            pltpu.VMEM((512, 128), jnp.float32),
            pltpu.SemaphoreType.DMA((NB,)),
        ],
        compiler_params=pltpu.CompilerParams(vmem_limit_bytes=32 * 2**20),
        cost_estimate=pl.CostEstimate(flops=5_000_000_000, bytes_accessed=8_000_000, transcendentals=2_200_000),
    )(place, block_owner, queries, absorb_value, *mine, *other)


def solution(mesh):
    return jax.shard_map(
        per_device,
        mesh=mesh,
        in_specs=(
            P(AXES, None),
            P(),
            P(AXES, None),
            P(None, "head"),
            P("head", None, None),
            P("head", None, None),
            P(),
        ),
        out_specs=P("ctx", "head"),
        check_vma=False,
    )
```

```python
import functools
import math

import jax
import jax.numpy as jnp
from jax import lax
from jax.experimental import pallas as pl
from jax.experimental.pallas import tpu as pltpu
from jax.sharding import PartitionSpec as P

QLAT = 1536
LATENT = 512
ROPE = 64
NOPE = 128
KV = LATENT + ROPE
HD = 4
HALF = 128
NB = 32
EPS = 1e-06
SCALE2 = float(NOPE + ROPE) ** (-0.5) * math.log2(math.e)
MASKED = -1e30
AXES = ("ctx", "head")
SHIFTS = (1, 3, 2)


def flat(x, y, z, c):
    x, y, z, c = x % 4, y % 4, z % 8, c % 2
    return (((y // 2) * 4 + x) * 2 + c) * 16 + (y % 2) * 8 + z


def move(a, to):
    pairs = []
    for x in range(4):
        for y in range(4):
            for z in range(8):
                for c in range(2):
                    pairs.append((flat(x, y, z, c), flat(*to(x, y, z, c))))
    return lax.ppermute(a, AXES, pairs)


def shift(k, first):
    def to(x, y, z, c):
        return (x + k, y, z, c) if (c == 0) == first else (x, y + k, z, c)

    return to


def swap_core(x, y, z, c):
    return (x, y, z, c + 1)


def turn_kernel(x_ref, out_ref):
    out_ref[...] = x_ref[...].reshape(HALF, KV).T


def project_kernel(q_ref, gain_ref, cos_ref, sin_ref, up_ref, ak_ref, out_ref):
    x = q_ref[...].astype(jnp.float32)
    ms = jnp.mean(x * x, axis=-1, keepdims=True)
    normed = (x * lax.rsqrt(ms + EPS) * gain_ref[...].astype(jnp.float32)).astype(jnp.bfloat16)
    proj = lax.dot_general(
        up_ref[...], normed, (((0,), (1,)), ((), ())), preferred_element_type=jnp.float32
    )
    cos, sin = cos_ref[...], sin_ref[...]
    for h in range(HD):
        base = h * (NOPE + ROPE)
        nope = proj[base : base + NOPE].astype(jnp.bfloat16)
        a = proj[base + NOPE : base + NOPE + ROPE // 2]
        b = proj[base + NOPE + ROPE // 2 : base + NOPE + ROPE]
        pe = jnp.concatenate([a * cos - b * sin, a * sin + b * cos], axis=0).astype(jnp.bfloat16)
        qa = lax.dot_general(
            ak_ref[h], nope, (((0,), (0,)), ((), ())), preferred_element_type=jnp.float32
        ).astype(jnp.bfloat16)
        for half in range(2):
            cols = slice(h * HALF, (h + 1) * HALF)
            out_ref[half, :LATENT, cols] = qa[:, half * HALF : (half + 1) * HALF]
            out_ref[half, LATENT:, cols] = pe[:, half * HALF : (half + 1) * HALF]


def attend_kernel(slots, first, last, place_ref, owner_ref, q_ref, *rest):
    rest = list(rest)
    if last:
        av_ref = rest.pop(0)
    if not first:
        acc_in, m_in, l_in = rest.pop(0), rest.pop(0), rest.pop(0)
    pieces = [rest.pop(0) for _ in slots]
    if last:
        out_ref = rest.pop(0)
        keys, acc, m_ref, l_ref, s_now, s_next, rank, bpos = rest
    else:
        acc, m_ref, l_ref = rest.pop(0), rest.pop(0), rest.pop(0)
        keys, s_now, s_next, rank, bpos = rest
    me_x, me_y, me_c = place_ref[0], place_ref[1], place_ref[2]

    where = []
    for b in range(NB):
        rank[b] = 0
    for far, second in slots:
        core = me_c if far == 0 else 1 - me_c
        for i in range(4):
            along = (0,) + SHIFTS
            dx = jnp.where(core == 0, along[i], second)
            dy = jnp.where(core == 0, second, along[i])
            x = (me_x - dx + 4) & 3
            y = (me_y - dy + 4) & 3
            p = owner_ref[(y >> 1) * 8 + x * 2 + core]
            b = jnp.where((y & 1) == 0, p, NB - 1 - p)
            rank[b] = 1
            where.append(b)
    mine = owner_ref[(me_y >> 1) * 8 + me_x * 2 + me_c]
    other = NB - 1 - mine
    count = jnp.int32(0)
    low = jnp.int32(0)
    high = jnp.int32(0)
    for b in range(NB):
        here = rank[b]
        rank[b] = count
        bpos[count] = b
        count = count + here
        low = low + jnp.where(b <= mine, here, 0)
        high = high + jnp.where(b <= other, here, 0)
    for s, b in enumerate(where):
        keys[rank[b]] = pieces[s // 4][s % 4]

    if first:
        acc[...] = jnp.zeros_like(acc)
        m_ref[...] = jnp.full_like(m_ref, MASKED)
        l_ref[...] = jnp.zeros_like(l_ref)
    else:
        acc[...] = acc_in[...]
        m_ref[...] = m_in[...]
        l_ref[...] = l_in[...]

    tiles_high = (high + 3) // 4
    tiles = tiles_high + (low + 3) // 4
    delta = (
        lax.broadcasted_iota(jnp.int32, (HALF, 512), 0)
        - (lax.broadcasted_iota(jnp.int32, (HALF, 512), 1) & (HALF - 1))
    )

    def at(t):
        is_high = t < tiles_high
        half = jnp.where(is_high, 1, 0)
        return half, jnp.where(is_high, t, t - tiles_high), jnp.where(is_high, other, mine)

    def load(j):
        return jnp.concatenate([keys[4 * j + i] for i in range(4)], axis=1)

    def score(t):
        half, j, a = at(t)
        s = lax.dot_general(
            load(j), q_ref[half], (((0,), (0,)), ((), ())), preferred_element_type=jnp.float32
        )
        return jnp.concatenate(
            [
                jnp.where(
                    delta <= (a - bpos[4 * j + i]) * HALF, s[i * HALF : (i + 1) * HALF], MASKED
                )
                for i in range(4)
            ],
            axis=0,
        )

    def update(t, s):
        half, j, _ = at(t)
        old = m_ref[half]
        new = jnp.maximum(old, jnp.max(s, axis=0, keepdims=True))
        w = jnp.exp2((s - new) * SCALE2)
        f = jnp.exp2((old - new) * SCALE2)
        m_ref[half] = new
        l_ref[half] = l_ref[half] * f + jnp.sum(w, axis=0, keepdims=True)
        acc[half] = acc[half] * f + jnp.dot(
            load(j)[:LATENT], w.astype(jnp.bfloat16), preferred_element_type=jnp.float32
        )

    @pl.when(tiles > 0)
    def _():
        s_now[...] = score(0)

    def step(t, _):
        s_next[...] = score(jnp.minimum(t + 1, tiles - 1))
        update(t, s_now[...])
        s_now[...] = s_next[...]
        return 0

    lax.fori_loop(0, tiles, step, 0)

    if last:
        for half in range(2):
            for h in range(HD):
                cols = slice(h * HALF, (h + 1) * HALF)
                lat = (acc[half, :, cols] / l_ref[half, :, cols]).astype(jnp.bfloat16)
                out_ref[half * HALF : (half + 1) * HALF, cols] = lax.dot_general(
                    lat, av_ref[h], (((0,), (0,)), ((), ())), preferred_element_type=jnp.float32
                ).astype(jnp.bfloat16)


VM = pl.BlockSpec(memory_space=pltpu.VMEM)
SM = pl.BlockSpec(memory_space=pltpu.SMEM)


def attend(place, block_owner, queries, pieces, slots, state=None, value=None):
    first, last = state is None, value is not None
    n = 4 * len(pieces)
    state_shapes = ((2, LATENT, 512), (2, 1, 512), (2, 1, 512))
    scratch = [pltpu.VMEM((n, KV, HALF), jnp.bfloat16)]
    if last:
        scratch += [pltpu.VMEM(s, jnp.float32) for s in state_shapes]
        out = jax.ShapeDtypeStruct((256, 512), jnp.bfloat16)
    else:
        out = [jax.ShapeDtypeStruct(s, jnp.float32) for s in state_shapes]
    scratch += [pltpu.VMEM((512, 512), jnp.float32)] * 2
    scratch += [pltpu.SMEM((NB,), jnp.int32), pltpu.SMEM((NB + 1,), jnp.int32)]
    args = [place, block_owner, queries]
    args += [value] if last else []
    args += [] if first else list(state)
    args += pieces
    return pl.pallas_call(
        functools.partial(attend_kernel, slots, first, last),
        out_shape=out,
        in_specs=[SM, SM] + [VM] * (len(args) - 2),
        out_specs=VM if last else [VM] * 3,
        scratch_shapes=scratch,
        compiler_params=pltpu.CompilerParams(vmem_limit_bytes=30 * 2**20),
        cost_estimate=pl.CostEstimate(
            flops=n * 150_000_000, bytes_accessed=n * 150_000, transcendentals=n * 70_000
        ),
    )(*args)


def per_device(query_latent, norm_gain, kv_latent, q_up, absorb_key, absorb_value, block_owner):
    ctx, head = lax.axis_index("ctx"), lax.axis_index("head")
    me_x, me_y, me_c = (ctx // 2) % 4, (ctx // 8) * 2 + head // 8, ctx % 2
    place = jnp.stack([me_x, me_y, me_c]).astype(jnp.int32)

    z_groups = [list(range(8)), list(range(8, 16))]
    own = lax.all_to_all(
        jnp.broadcast_to(kv_latent[None], (8,) + kv_latent.shape),
        "head", 0, 0, axis_index_groups=z_groups, tiled=True,
    )
    own = pl.pallas_call(
        turn_kernel,
        out_shape=jax.ShapeDtypeStruct((KV, HALF), jnp.bfloat16),
        in_specs=[VM],
        out_specs=VM,
    )(own)
    ring = jnp.stack([own] + [move(own, shift(k, True)) for k in SHIFTS], axis=0)
    near = [ring] + [move(ring, shift(k, False)) for k in SHIFTS]
    distant = [move(t, swap_core) for t in near]

    rows = lax.all_to_all(
        jnp.broadcast_to(query_latent[None], (16,) + query_latent.shape),
        "head", 0, 0, tiled=True,
    ).reshape(256, QLAT)
    p = block_owner[ctx]
    offset = jnp.arange(256, dtype=jnp.int32)
    pos = jnp.where(offset < HALF, p * HALF + offset, (NB - 1 - p) * HALF + offset - HALF)
    freq = jnp.exp(jnp.arange(ROPE // 2, dtype=jnp.float32) * (-math.log(10000.0) / (ROPE // 2)))
    angles = freq[:, None] * pos.astype(jnp.float32)
    queries = pl.pallas_call(
        project_kernel,
        out_shape=jax.ShapeDtypeStruct((2, KV, 512), jnp.bfloat16),
        in_specs=[VM] * 6,
        out_specs=VM,
        compiler_params=pltpu.CompilerParams(vmem_limit_bytes=24 * 2**20),
        cost_estimate=pl.CostEstimate(flops=750_000_000, bytes_accessed=5_000_000, transcendentals=0),
    )(rows, norm_gain.reshape(1, QLAT), jnp.cos(angles), jnp.sin(angles), q_up, absorb_key)

    shifts = (0,) + SHIFTS
    slots = tuple((far, k) for far in range(2) for k in shifts)
    return attend(place, block_owner, queries, near + distant, slots, value=absorb_value)


def solution(mesh):
    return jax.shard_map(
        per_device,
        mesh=mesh,
        in_specs=(
            P(AXES, None),
            P(),
            P(AXES, None),
            P(None, "head"),
            P("head", None, None),
            P("head", None, None),
            P(),
        ),
        out_specs=P("ctx", "head"),
        check_vma=False,
    )
```

```python
import functools
import math

import jax
import jax.numpy as jnp
from jax import lax
from jax.experimental import pallas as pl
from jax.experimental.pallas import tpu as pltpu
from jax.sharding import PartitionSpec as P

QLAT = 1536
LATENT = 512
ROPE = 64
NOPE = 128
KV = LATENT + ROPE
HD = 4
HALF = 128
NB = 32
EPS = 1e-06
SCALE2 = float(NOPE + ROPE) ** (-0.5) * math.log2(math.e)
MASKED = -1e30
AXES = ("ctx", "head")
SHIFTS = (1, 3, 2)


def flat(x, y, z, c):
    x, y, z, c = x % 4, y % 4, z % 8, c % 2
    return (((y // 2) * 4 + x) * 2 + c) * 16 + (y % 2) * 8 + z


def move(a, to):
    pairs = []
    for x in range(4):
        for y in range(4):
            for z in range(8):
                for c in range(2):
                    pairs.append((flat(x, y, z, c), flat(*to(x, y, z, c))))
    return lax.ppermute(a, AXES, pairs)


def shift(k, first):
    def to(x, y, z, c):
        return (x + k, y, z, c) if (c == 0) == first else (x, y + k, z, c)

    return to


def swap_core(x, y, z, c):
    return (x, y, z, c + 1)


def spread_kernel(q_ref, q_out):
    q_out[...] = jnp.broadcast_to(q_ref[...][None], q_out.shape)


def turn_kernel(*refs):
    for i in range(4):
        refs[4][i] = refs[i][...].T


def gate_kernel(_x, _token, _out):
    pass


def project_kernel(q_ref, gain_ref, cos_ref, sin_ref, up_ref, ak_ref, out_ref):
    x = q_ref[...].astype(jnp.float32)
    ms = jnp.mean(x * x, axis=-1, keepdims=True)
    normed = (x * lax.rsqrt(ms + EPS) * gain_ref[...].astype(jnp.float32)).astype(jnp.bfloat16)
    proj = lax.dot_general(
        up_ref[...], normed, (((0,), (1,)), ((), ())), preferred_element_type=jnp.float32
    )
    cos, sin = cos_ref[...], sin_ref[...]
    for h in range(HD):
        base = h * (NOPE + ROPE)
        nope = proj[base : base + NOPE].astype(jnp.bfloat16)
        a = proj[base + NOPE : base + NOPE + ROPE // 2]
        b = proj[base + NOPE + ROPE // 2 : base + NOPE + ROPE]
        pe = jnp.concatenate([a * cos - b * sin, a * sin + b * cos], axis=0).astype(jnp.bfloat16)
        qa = lax.dot_general(
            ak_ref[h], nope, (((0,), (0,)), ((), ())), preferred_element_type=jnp.float32
        ).astype(jnp.bfloat16)
        for half in range(2):
            cols = slice(h * HALF, (h + 1) * HALF)
            out_ref[half, :LATENT, cols] = qa[:, half * HALF : (half + 1) * HALF]
            out_ref[half, LATENT:, cols] = pe[:, half * HALF : (half + 1) * HALF]


def attend_kernel(slots, first, last, place_ref, owner_ref, q_ref, *rest):
    rest = list(rest)
    if last:
        av_src = rest.pop(0)
    if not first:
        state = [rest.pop(0) for _ in range(3)]
    pieces = [rest.pop(0) for _ in slots]
    if last:
        out_ref = rest.pop(0)
    else:
        state = [rest.pop(0) for _ in range(3)]
    keys = rest.pop(0)
    if first and last:
        state = [rest.pop(0) for _ in range(3)]
    acc, m_ref, l_ref = state
    s_now, s_next, rank, bpos = rest[:4]
    if last:
        av_ref, av_sem = rest[4:]
        av_copy = pltpu.make_async_copy(av_src, av_ref, av_sem)
        av_copy.start()
    me_x, me_y, me_c = place_ref[0], place_ref[1], place_ref[2]

    where = []
    for b in range(NB):
        rank[b] = 0
    along = (0,) + SHIFTS
    for far, second in slots:
        core = me_c if far == 0 else 1 - me_c
        for i in range(4):
            dx = jnp.where(core == 0, along[i], second)
            dy = jnp.where(core == 0, second, along[i])
            x = (me_x - dx + 4) & 3
            y = (me_y - dy + 4) & 3
            p = owner_ref[(y >> 1) * 8 + x * 2 + core]
            b = jnp.where((y & 1) == 0, p, NB - 1 - p)
            rank[b] = 1
            where.append(b)
    mine = owner_ref[(me_y >> 1) * 8 + me_x * 2 + me_c]
    other = NB - 1 - mine
    count = jnp.int32(0)
    low = jnp.int32(0)
    high = jnp.int32(0)
    for b in range(NB):
        here = rank[b]
        rank[b] = count
        bpos[count] = b
        count = count + here
        low = low + jnp.where(b <= mine, here, 0)
        high = high + jnp.where(b <= other, here, 0)
    for s, b in enumerate(where):
        keys[rank[b]] = pieces[s // 4][s % 4]

    if first:
        acc[...] = jnp.zeros_like(acc)
        m_ref[...] = jnp.full_like(m_ref, MASKED)
        l_ref[...] = jnp.zeros_like(l_ref)

    tiles_high = (high + 3) // 4
    tiles = tiles_high + (low + 3) // 4
    delta = (
        lax.broadcasted_iota(jnp.int32, (HALF, 512), 0)
        - (lax.broadcasted_iota(jnp.int32, (HALF, 512), 1) & (HALF - 1))
    )

    def at(t):
        is_high = t < tiles_high
        half = jnp.where(is_high, 1, 0)
        return half, jnp.where(is_high, t, t - tiles_high), jnp.where(is_high, other, mine)

    def load(j):
        return jnp.concatenate([keys[4 * j + i] for i in range(4)], axis=1)

    def score(t):
        half, j, a = at(t)
        s = lax.dot_general(
            load(j), q_ref[half], (((0,), (0,)), ((), ())), preferred_element_type=jnp.float32
        )
        return jnp.concatenate(
            [
                jnp.where(
                    delta <= (a - bpos[4 * j + i]) * HALF, s[i * HALF : (i + 1) * HALF], MASKED
                )
                for i in range(4)
            ],
            axis=0,
        )

    def update(t, s):
        half, j, _ = at(t)
        old = m_ref[half]
        new = jnp.maximum(old, jnp.max(s, axis=0, keepdims=True))
        w = jnp.exp2((s - new) * SCALE2)
        f = jnp.exp2((old - new) * SCALE2)
        m_ref[half] = new
        l_ref[half] = l_ref[half] * f + jnp.sum(w, axis=0, keepdims=True)
        acc[half] = acc[half] * f + jnp.dot(
            load(j)[:LATENT], w.astype(jnp.bfloat16), preferred_element_type=jnp.float32
        )

    @pl.when(tiles > 0)
    def _():
        s_now[...] = score(0)

    def step(t, _):
        s_next[...] = score(jnp.minimum(t + 1, tiles - 1))
        update(t, s_now[...])
        s_now[...] = s_next[...]
        return 0

    lax.fori_loop(0, tiles, step, 0)

    if last:
        av_copy.wait()
        for half in range(2):
            for h in range(HD):
                cols = slice(h * HALF, (h + 1) * HALF)
                lat = (acc[half, :, cols] / l_ref[half, :, cols]).astype(jnp.bfloat16)
                out_ref[half * HALF : (half + 1) * HALF, cols] = lax.dot_general(
                    lat, av_ref[h], (((0,), (0,)), ((), ())), preferred_element_type=jnp.float32
                ).astype(jnp.bfloat16)


VM = pl.BlockSpec(memory_space=pltpu.VMEM)
SM = pl.BlockSpec(memory_space=pltpu.SMEM)
FREE = pl.BlockSpec(memory_space=pl.ANY)


def after(x, token):
    return pl.pallas_call(
        gate_kernel,
        out_shape=jax.ShapeDtypeStruct(x.shape, x.dtype),
        in_specs=[FREE, FREE],
        out_specs=FREE,
        input_output_aliases={0: 0},
        compiler_params=pltpu.CompilerParams(vmem_limit_bytes=2**20),
        cost_estimate=pl.CostEstimate(flops=1000, bytes_accessed=1000, transcendentals=0),
    )(x, token)


def attend(place, block_owner, queries, pieces, slots, state=None, value=None):
    first, last = state is None, value is not None
    n = 4 * len(pieces)
    state_shapes = ((2, LATENT, 512), (2, 1, 512), (2, 1, 512))
    scratch = [pltpu.VMEM((n, KV, HALF), jnp.bfloat16)]
    aliases = {}
    if last and first:
        scratch += [pltpu.VMEM(s, jnp.float32) for s in state_shapes]
    if last:
        out = jax.ShapeDtypeStruct((256, 512), jnp.bfloat16)
    else:
        out = [jax.ShapeDtypeStruct(s, jnp.float32) for s in state_shapes]
    scratch += [pltpu.VMEM((512, 512), jnp.float32)] * 2
    scratch += [pltpu.SMEM((NB,), jnp.int32), pltpu.SMEM((NB + 1,), jnp.int32)]
    if last:
        scratch += [pltpu.VMEM((HD, LATENT, 128), jnp.bfloat16), pltpu.SemaphoreType.DMA]
    specs = [SM, SM, VM] + ([FREE] if last else [])
    args = [place, block_owner, queries]
    args += [value] if last else []
    if not (first or last):
        aliases = {len(args) + i: i for i in range(3)}
    args += [] if first else list(state)
    args += pieces
    return pl.pallas_call(
        functools.partial(attend_kernel, slots, first, last),
        out_shape=out,
        in_specs=specs + [VM] * (len(args) - len(specs)),
        out_specs=VM if last else [VM] * 3,
        scratch_shapes=scratch,
        input_output_aliases=aliases,
        compiler_params=pltpu.CompilerParams(vmem_limit_bytes=16 * 2**20),
        cost_estimate=pl.CostEstimate(
            flops=n * 1_000_000, bytes_accessed=n * 1_000, transcendentals=0
        ),
    )(*args)


def per_device(query_latent, norm_gain, kv_latent, q_up, absorb_key, absorb_value, block_owner):
    ctx, head = lax.axis_index("ctx"), lax.axis_index("head")
    me_x, me_y, me_c = (ctx // 2) % 4, (ctx // 8) * 2 + head // 8, ctx % 2
    place = jnp.stack([me_x, me_y, me_c]).astype(jnp.int32)

    q_spread = pl.pallas_call(
        spread_kernel,
        out_shape=jax.ShapeDtypeStruct((16,) + query_latent.shape, jnp.bfloat16),
        in_specs=[VM],
        out_specs=VM,
        compiler_params=pltpu.CompilerParams(vmem_limit_bytes=4 * 2**20),
    )(query_latent)

    own = lax.all_to_all(
        jnp.broadcast_to(kv_latent[None], (8,) + kv_latent.shape),
        "head", 0, 0, axis_index_groups=[list(range(8)), list(range(8, 16))], tiled=True
    ).reshape(HALF, KV)

    rows = lax.all_to_all(q_spread, "head", 0, 0, tiled=True).reshape(256, QLAT)

    blocks = [own] + [move(own, shift(k, True)) for k in SHIFTS]
    stack = pl.pallas_call(
        turn_kernel,
        out_shape=jax.ShapeDtypeStruct((4, KV, HALF), jnp.bfloat16),
        in_specs=[VM] * 4,
        out_specs=VM,
        compiler_params=pltpu.CompilerParams(vmem_limit_bytes=8 * 2**20),
    )(*blocks)
    near = {0: stack}
    for k in SHIFTS:
        near[k] = move(stack, shift(k, False))
    p = block_owner[ctx]
    offset = jnp.arange(256, dtype=jnp.int32)
    pos = jnp.where(offset < HALF, p * HALF + offset, (NB - 1 - p) * HALF + offset - HALF)
    freq = jnp.exp(jnp.arange(ROPE // 2, dtype=jnp.float32) * (-math.log(10000.0) / (ROPE // 2)))
    angles = freq[:, None] * pos.astype(jnp.float32)
    queries = pl.pallas_call(
        project_kernel,
        out_shape=jax.ShapeDtypeStruct((2, KV, 512), jnp.bfloat16),
        in_specs=[VM] * 6,
        out_specs=VM,
        compiler_params=pltpu.CompilerParams(vmem_limit_bytes=16 * 2**20),
        cost_estimate=pl.CostEstimate(flops=750_000_000, bytes_accessed=5_000_000, transcendentals=0),
    )(rows, norm_gain.reshape(1, QLAT), jnp.cos(angles), jnp.sin(angles), q_up, absorb_key)

    distant = {0: move(stack, swap_core)}

    def part(keys, **more):
        pieces = [near[k] for k in keys] + [distant[k] for k in keys]
        kinds = tuple((far, k) for far in range(2) for k in keys)
        return attend(place, block_owner, queries, pieces, kinds, **more)

    state = part([0])
    for k in SHIFTS:
        near[k] = after(near[k], state[1])
        distant[k] = move(near[k], swap_core)
    return part([1, 3, 2], state=state, value=absorb_value)


def solution(mesh):
    return jax.shard_map(
        per_device,
        mesh=mesh,
        in_specs=(
            P(AXES, None),
            P(),
            P(AXES, None),
            P(None, "head"),
            P("head", None, None),
            P("head", None, None),
            P(),
        ),
        out_specs=P("ctx", "head"),
        check_vma=False,
    )
```

```python
import functools
import math

import jax
import jax.numpy as jnp
from jax import lax
from jax.experimental import pallas as pl
from jax.experimental.pallas import tpu as pltpu
from jax.sharding import PartitionSpec as P

QLAT = 1536
LATENT = 512
ROPE = 64
NOPE = 128
KV = LATENT + ROPE
HD = 4
HALF = 128
NB = 32
EPS = 1e-06
SCALE2 = float(NOPE + ROPE) ** (-0.5) * math.log2(math.e)
MASKED = -1e30
AXES = ("ctx", "head")
SHIFTS = (2, 3, 1)


def flat(x, y, z, c):
    x, y, z, c = x % 4, y % 4, z % 8, c % 2
    return (((y // 2) * 4 + x) * 2 + c) * 16 + (y % 2) * 8 + z


def move(a, to):
    pairs = []
    for x in range(4):
        for y in range(4):
            for z in range(8):
                for c in range(2):
                    pairs.append((flat(x, y, z, c), flat(*to(x, y, z, c))))
    return lax.ppermute(a, AXES, pairs)


def shift(k, first):
    def to(x, y, z, c):
        return (x + k, y, z, c) if (c == 0) == first else (x, y + k, z, c)

    return to


def swap_row(x, y, z, c):
    return (x, y ^ 1, z, c)


def swap_core(x, y, z, c):
    return (x, y, z, c + 1)


def spread_kernel(q_ref, pair_ref, q_out):
    both = jnp.concatenate([q_ref[...], pair_ref[...]], axis=0)
    q_out[...] = jnp.broadcast_to(both[None], q_out.shape)


def turn_kernel(*refs):
    for i in range(4):
        refs[4][i] = refs[i][...].T


def gate_kernel(_x, _token, _out):
    pass


def project_kernel(place_ref, q_ref, gain_ref, cos_ref, sin_ref, up_ref, ak_ref, out_ref):
    own = place_ref[1] & 1
    x = jnp.concatenate(
        [q_ref[:, 16 * k : 16 * k + 16].reshape(HALF, QLAT) for k in range(2)], axis=0
    ).astype(jnp.float32)
    ms = jnp.mean(x * x, axis=-1, keepdims=True)
    normed = (x * lax.rsqrt(ms + EPS) * gain_ref[...].astype(jnp.float32)).astype(jnp.bfloat16)
    proj = lax.dot_general(
        up_ref[...], normed, (((0,), (1,)), ((), ())), preferred_element_type=jnp.float32
    )
    cos, sin = cos_ref[...], sin_ref[...]
    for h in range(HD):
        base = h * (NOPE + ROPE)
        nope = proj[base : base + NOPE].astype(jnp.bfloat16)
        a = proj[base + NOPE : base + NOPE + ROPE // 2]
        b = proj[base + NOPE + ROPE // 2 : base + NOPE + ROPE]
        pe = jnp.concatenate([a * cos - b * sin, a * sin + b * cos], axis=0).astype(jnp.bfloat16)
        qa = lax.dot_general(
            ak_ref[h], nope, (((0,), (0,)), ((), ())), preferred_element_type=jnp.float32
        ).astype(jnp.bfloat16)
        for k in range(2):
            half = own if k == 0 else 1 - own
            cols = slice(h * HALF, (h + 1) * HALF)
            out_ref[half, :LATENT, cols] = qa[:, k * HALF : (k + 1) * HALF]
            out_ref[half, LATENT:, cols] = pe[:, k * HALF : (k + 1) * HALF]


def attend_kernel(slots, first, last, place_ref, owner_ref, q_ref, *rest):
    rest = list(rest)
    if last:
        av_src = rest.pop(0)
    if not first:
        state = [rest.pop(0) for _ in range(3)]
    pieces = [rest.pop(0) for _ in slots]
    if last:
        out_ref = rest.pop(0)
    else:
        state = [rest.pop(0) for _ in range(3)]
    keys = rest.pop(0)
    if first and last:
        state = [rest.pop(0) for _ in range(3)]
    acc, m_ref, l_ref = state
    s_now, s_next, rank, bpos = rest[:4]
    if last:
        av_ref, av_sem = rest[4:]
        av_copy = pltpu.make_async_copy(av_src, av_ref, av_sem)
        av_copy.start()
    me_x, me_y, me_c = place_ref[0], place_ref[1], place_ref[2]

    where = []
    for b in range(NB):
        rank[b] = 0
    along = (0,) + SHIFTS
    for far, second in slots:
        core = me_c if far == 0 else 1 - me_c
        for i in range(4):
            dx = jnp.where(core == 0, along[i], second)
            dy = jnp.where(core == 0, second, along[i])
            x = (me_x - dx + 4) & 3
            y = (me_y - dy + 4) & 3
            p = owner_ref[(y >> 1) * 8 + x * 2 + core]
            b = jnp.where((y & 1) == 0, p, NB - 1 - p)
            rank[b] = 1
            where.append(b)
    mine = owner_ref[(me_y >> 1) * 8 + me_x * 2 + me_c]
    other = NB - 1 - mine
    count = jnp.int32(0)
    low = jnp.int32(0)
    high = jnp.int32(0)
    for b in range(NB):
        here = rank[b]
        rank[b] = count
        bpos[count] = b
        count = count + here
        low = low + jnp.where(b <= mine, here, 0)
        high = high + jnp.where(b <= other, here, 0)
    for s, b in enumerate(where):
        keys[rank[b]] = pieces[s // 4][s % 4]

    if first:
        acc[...] = jnp.zeros_like(acc)
        m_ref[...] = jnp.full_like(m_ref, MASKED)
        l_ref[...] = jnp.zeros_like(l_ref)

    tiles_high = (high + 3) // 4
    tiles = tiles_high + (low + 3) // 4
    delta = (
        lax.broadcasted_iota(jnp.int32, (HALF, 512), 0)
        - (lax.broadcasted_iota(jnp.int32, (HALF, 512), 1) & (HALF - 1))
    )

    def at(t):
        is_high = t < tiles_high
        half = jnp.where(is_high, 1, 0)
        return half, jnp.where(is_high, t, t - tiles_high), jnp.where(is_high, other, mine)

    def load(j):
        return jnp.concatenate([keys[4 * j + i] for i in range(4)], axis=1)

    def score(t):
        half, j, a = at(t)
        s = lax.dot_general(
            load(j), q_ref[half], (((0,), (0,)), ((), ())), preferred_element_type=jnp.float32
        )
        return jnp.concatenate(
            [
                jnp.where(
                    delta <= (a - bpos[4 * j + i]) * HALF, s[i * HALF : (i + 1) * HALF], MASKED
                )
                for i in range(4)
            ],
            axis=0,
        )

    def update(t, s):
        half, j, _ = at(t)
        old = m_ref[half]
        new = jnp.maximum(old, jnp.max(s, axis=0, keepdims=True))
        w = jnp.exp2((s - new) * SCALE2)
        f = jnp.exp2((old - new) * SCALE2)
        m_ref[half] = new
        l_ref[half] = l_ref[half] * f + jnp.sum(w, axis=0, keepdims=True)
        acc[half] = acc[half] * f + jnp.dot(
            load(j)[:LATENT], w.astype(jnp.bfloat16), preferred_element_type=jnp.float32
        )

    @pl.when(tiles > 0)
    def _():
        s_now[...] = score(0)

    def step(t, _):
        s_next[...] = score(t + 1)
        update(t, s_now[...])
        s_now[...] = s_next[...]
        return 0

    lax.fori_loop(0, tiles - 1, step, 0)

    @pl.when(tiles > 0)
    def _():
        update(tiles - 1, s_now[...])

    if last:
        av_copy.wait()
        for half in range(2):
            for h in range(HD):
                cols = slice(h * HALF, (h + 1) * HALF)
                lat = (acc[half, :, cols] / l_ref[half, :, cols]).astype(jnp.bfloat16)
                out_ref[half * HALF : (half + 1) * HALF, cols] = lax.dot_general(
                    lat, av_ref[h], (((0,), (0,)), ((), ())), preferred_element_type=jnp.float32
                ).astype(jnp.bfloat16)


VM = pl.BlockSpec(memory_space=pltpu.VMEM)
SM = pl.BlockSpec(memory_space=pltpu.SMEM)
FREE = pl.BlockSpec(memory_space=pl.ANY)


def after(x, token):
    return pl.pallas_call(
        gate_kernel,
        out_shape=jax.ShapeDtypeStruct(x.shape, x.dtype),
        in_specs=[FREE, FREE],
        out_specs=FREE,
        input_output_aliases={0: 0},
        compiler_params=pltpu.CompilerParams(vmem_limit_bytes=2**20),
        cost_estimate=pl.CostEstimate(flops=1000, bytes_accessed=1000, transcendentals=0),
    )(x, token)


def attend(place, block_owner, queries, pieces, slots, state=None, value=None):
    first, last = state is None, value is not None
    n = 4 * len(pieces)
    state_shapes = ((2, LATENT, 512), (2, 1, 512), (2, 1, 512))
    scratch = [pltpu.VMEM((n, KV, HALF), jnp.bfloat16)]
    aliases = {}
    if last and first:
        scratch += [pltpu.VMEM(s, jnp.float32) for s in state_shapes]
    if last:
        out = jax.ShapeDtypeStruct((256, 512), jnp.bfloat16)
    else:
        out = [jax.ShapeDtypeStruct(s, jnp.float32) for s in state_shapes]
    scratch += [pltpu.VMEM((512, 512), jnp.float32)] * 2
    scratch += [pltpu.SMEM((NB,), jnp.int32), pltpu.SMEM((NB + 1,), jnp.int32)]
    if last:
        scratch += [pltpu.VMEM((HD, LATENT, 128), jnp.bfloat16), pltpu.SemaphoreType.DMA]
    specs = [SM, SM, VM] + ([FREE] if last else [])
    args = [place, block_owner, queries]
    args += [value] if last else []
    if not (first or last):
        aliases = {len(args) + i: i for i in range(3)}
    args += [] if first else list(state)
    args += pieces
    return pl.pallas_call(
        functools.partial(attend_kernel, slots, first, last),
        out_shape=out,
        in_specs=specs + [VM] * (len(args) - len(specs)),
        out_specs=VM if last else [VM] * 3,
        scratch_shapes=scratch,
        input_output_aliases=aliases,
        compiler_params=pltpu.CompilerParams(vmem_limit_bytes=16 * 2**20),
        cost_estimate=pl.CostEstimate(
            flops=n * 1_000_000, bytes_accessed=n * 1_000, transcendentals=0
        ),
    )(*args)


def per_device(query_latent, norm_gain, kv_latent, q_up, absorb_key, absorb_value, block_owner):
    ctx, head = lax.axis_index("ctx"), lax.axis_index("head")
    me_x, me_y, me_c = (ctx // 2) % 4, (ctx // 8) * 2 + head // 8, ctx % 2
    place = jnp.stack([me_x, me_y, me_c]).astype(jnp.int32)

    z_groups = [list(range(8)), list(range(8, 16))]
    q_spread = pl.pallas_call(
        spread_kernel,
        out_shape=jax.ShapeDtypeStruct((8, 32, QLAT), jnp.bfloat16),
        in_specs=[VM] * 2,
        out_specs=VM,
        compiler_params=pltpu.CompilerParams(vmem_limit_bytes=4 * 2**20),
    )(query_latent, move(query_latent, swap_row))

    own = lax.all_to_all(
        jnp.broadcast_to(kv_latent[None], (8,) + kv_latent.shape),
        "head", 0, 0, axis_index_groups=z_groups, tiled=True
    ).reshape(HALF, KV)

    rows = lax.all_to_all(q_spread, "head", 0, 0, axis_index_groups=z_groups, tiled=True)

    blocks = [own] + [move(own, shift(k, True)) for k in SHIFTS]
    stack = pl.pallas_call(
        turn_kernel,
        out_shape=jax.ShapeDtypeStruct((4, KV, HALF), jnp.bfloat16),
        in_specs=[VM] * 4,
        out_specs=VM,
        compiler_params=pltpu.CompilerParams(vmem_limit_bytes=8 * 2**20),
    )(*blocks)
    near = {0: stack}
    for k in SHIFTS:
        near[k] = move(stack, shift(k, False))
    p = block_owner[ctx]
    offset = jnp.arange(256, dtype=jnp.int32)
    in_low = (offset < HALF) == (me_y % 2 == 0)
    pos = jnp.where(in_low, p, NB - 1 - p) * HALF + (offset & (HALF - 1))
    freq = jnp.exp(jnp.arange(ROPE // 2, dtype=jnp.float32) * (-math.log(10000.0) / (ROPE // 2)))
    angles = freq[:, None] * pos.astype(jnp.float32)
    queries = pl.pallas_call(
        project_kernel,
        out_shape=jax.ShapeDtypeStruct((2, KV, 512), jnp.bfloat16),
        in_specs=[SM] + [VM] * 6,
        out_specs=VM,
        compiler_params=pltpu.CompilerParams(vmem_limit_bytes=16 * 2**20),
        cost_estimate=pl.CostEstimate(flops=750_000_000, bytes_accessed=5_000_000, transcendentals=0),
    )(place, rows, norm_gain.reshape(1, QLAT), jnp.cos(angles), jnp.sin(angles), q_up, absorb_key)

    distant = {0: move(stack, swap_core)}

    def part(keys, **more):
        pieces = [near[k] for k in keys] + [distant[k] for k in keys]
        kinds = tuple((far, k) for far in range(2) for k in keys)
        return attend(place, block_owner, queries, pieces, kinds, **more)

    state = part([0])
    for k in SHIFTS:
        near[k] = after(near[k], state[1])
        distant[k] = move(near[k], swap_core)
    return part([1, 3, 2], state=state, value=absorb_value)


def solution(mesh):
    return jax.shard_map(
        per_device,
        mesh=mesh,
        in_specs=(
            P(AXES, None),
            P(),
            P(AXES, None),
            P(None, "head"),
            P("head", None, None),
            P("head", None, None),
            P(),
        ),
        out_specs=P("ctx", "head"),
        check_vma=False,
    )
```

```python
import functools
import math

import jax
import jax.numpy as jnp
from jax import lax
from jax.experimental import pallas as pl
from jax.experimental.pallas import tpu as pltpu
from jax.sharding import PartitionSpec as P

QLAT = 1536
LATENT = 512
ROPE = 64
NOPE = 128
KV = LATENT + ROPE
HD = 4
HALF = 128
NB = 32
EPS = 1e-06
SCALE2 = float(NOPE + ROPE) ** (-0.5) * math.log2(math.e)
MASKED = -1e30
AXES = ("ctx", "head")
SHIFTS = (2, 3, 1)


def flat(x, y, z, c):
    x, y, z, c = x % 4, y % 4, z % 8, c % 2
    return (((y // 2) * 4 + x) * 2 + c) * 16 + (y % 2) * 8 + z


def move(a, to):
    pairs = []
    for x in range(4):
        for y in range(4):
            for z in range(8):
                for c in range(2):
                    pairs.append((flat(x, y, z, c), flat(*to(x, y, z, c))))
    return lax.ppermute(a, AXES, pairs)


def shift(k, first):
    def to(x, y, z, c):
        return (x + k, y, z, c) if (c == 0) == first else (x, y + k, z, c)

    return to


def swap_row(x, y, z, c):
    return (x, y ^ 1, z, c)


def swap_core(x, y, z, c):
    return (x, y, z, c + 1)


def spread_kernel(q_ref, pair_ref, q_out):
    both = jnp.concatenate([q_ref[...], pair_ref[...]], axis=0)
    q_out[...] = jnp.broadcast_to(both[None], q_out.shape)


def turn_kernel(*refs):
    for i in range(4):
        refs[4][i] = refs[i][...].T


def gate_kernel(_x, _token, _out):
    pass


def project_kernel(
    place_ref, q_ref, gain_ref, cos_ref, sin_ref, up_src, ak_src, out_ref, up_ref, ak_ref, sems
):
    parts = [pl.ds(i * QLAT // 8, QLAT // 8) for i in range(8)]
    up_copies = [
        pltpu.make_async_copy(up_src.at[r], up_ref.at[r], sems.at[i]) for i, r in enumerate(parts)
    ]
    ak_copies = [
        pltpu.make_async_copy(ak_src.at[h], ak_ref.at[h], sems.at[8 + h]) for h in range(HD)
    ]
    for c in up_copies + ak_copies:
        c.start()
    own = place_ref[1] & 1
    x = jnp.concatenate(
        [q_ref[:, 16 * k : 16 * k + 16].reshape(HALF, QLAT) for k in range(2)], axis=0
    ).astype(jnp.float32)
    ms = jnp.mean(x * x, axis=-1, keepdims=True)
    normed = (x * lax.rsqrt(ms + EPS) * gain_ref[...].astype(jnp.float32)).astype(jnp.bfloat16)
    for c in up_copies + ak_copies:
        c.wait()
    proj = lax.dot_general(
        up_ref[...], normed, (((0,), (1,)), ((), ())), preferred_element_type=jnp.float32
    )
    cos, sin = cos_ref[...], sin_ref[...]
    for h in range(HD):
        base = h * (NOPE + ROPE)
        nope = proj[base : base + NOPE].astype(jnp.bfloat16)
        a = proj[base + NOPE : base + NOPE + ROPE // 2]
        b = proj[base + NOPE + ROPE // 2 : base + NOPE + ROPE]
        pe = jnp.concatenate([a * cos - b * sin, a * sin + b * cos], axis=0).astype(jnp.bfloat16)
        qa = lax.dot_general(
            ak_ref[h], nope, (((0,), (0,)), ((), ())), preferred_element_type=jnp.float32
        ).astype(jnp.bfloat16)
        for k in range(2):
            half = own if k == 0 else 1 - own
            cols = slice(h * HALF, (h + 1) * HALF)
            out_ref[half, :LATENT, cols] = qa[:, k * HALF : (k + 1) * HALF]
            out_ref[half, LATENT:, cols] = pe[:, k * HALF : (k + 1) * HALF]


def attend_kernel(slots, first, last, place_ref, owner_ref, q_ref, *rest):
    rest = list(rest)
    if last:
        av_src = rest.pop(0)
    if not first:
        state = [rest.pop(0) for _ in range(3)]
    pieces = [rest.pop(0) for _ in slots]
    if last:
        out_ref = rest.pop(0)
    else:
        state = [rest.pop(0) for _ in range(3)]
    keys = rest.pop(0)
    if first and last:
        state = [rest.pop(0) for _ in range(3)]
    acc, m_ref, l_ref = state
    s_now, s_next, rank, bpos = rest[:4]
    if last:
        av_ref, av_sem = rest[4:]
        av_copy = pltpu.make_async_copy(av_src, av_ref, av_sem)
        av_copy.start()
    me_x, me_y, me_c = place_ref[0], place_ref[1], place_ref[2]

    where = []
    for b in range(NB):
        rank[b] = 0
    along = (0,) + SHIFTS
    for far, second in slots:
        core = me_c if far == 0 else 1 - me_c
        for i in range(4):
            dx = jnp.where(core == 0, along[i], second)
            dy = jnp.where(core == 0, second, along[i])
            x = (me_x - dx + 4) & 3
            y = (me_y - dy + 4) & 3
            p = owner_ref[(y >> 1) * 8 + x * 2 + core]
            b = jnp.where((y & 1) == 0, p, NB - 1 - p)
            rank[b] = 1
            where.append(b)
    mine = owner_ref[(me_y >> 1) * 8 + me_x * 2 + me_c]
    other = NB - 1 - mine
    count = jnp.int32(0)
    low = jnp.int32(0)
    high = jnp.int32(0)
    for b in range(NB):
        here = rank[b]
        rank[b] = count
        bpos[count] = b
        count = count + here
        low = low + jnp.where(b <= mine, here, 0)
        high = high + jnp.where(b <= other, here, 0)
    for s, b in enumerate(where):
        keys[rank[b]] = pieces[s // 4][s % 4]

    if first:
        acc[...] = jnp.zeros_like(acc)
        m_ref[...] = jnp.full_like(m_ref, MASKED)
        l_ref[...] = jnp.zeros_like(l_ref)

    tiles_high = (high + 3) // 4
    tiles = tiles_high + (low + 3) // 4
    delta = (
        lax.broadcasted_iota(jnp.int32, (HALF, 512), 0)
        - (lax.broadcasted_iota(jnp.int32, (HALF, 512), 1) & (HALF - 1))
    )

    def at(t):
        is_high = t < tiles_high
        half = jnp.where(is_high, 1, 0)
        return half, jnp.where(is_high, t, t - tiles_high), jnp.where(is_high, other, mine)

    def load(j):
        return jnp.concatenate([keys[4 * j + i] for i in range(4)], axis=1)

    def score(t):
        half, j, a = at(t)
        s = lax.dot_general(
            load(j), q_ref[half], (((0,), (0,)), ((), ())), preferred_element_type=jnp.float32
        )
        return jnp.concatenate(
            [
                jnp.where(
                    delta <= (a - bpos[4 * j + i]) * HALF, s[i * HALF : (i + 1) * HALF], MASKED
                )
                for i in range(4)
            ],
            axis=0,
        )

    def update(t, s):
        half, j, _ = at(t)
        old = m_ref[half]
        new = jnp.maximum(old, jnp.max(s, axis=0, keepdims=True))
        w = jnp.exp2((s - new) * SCALE2)
        f = jnp.exp2((old - new) * SCALE2)
        m_ref[half] = new
        l_ref[half] = l_ref[half] * f + jnp.sum(w, axis=0, keepdims=True)
        acc[half] = acc[half] * f + jnp.dot(
            load(j)[:LATENT], w.astype(jnp.bfloat16), preferred_element_type=jnp.float32
        )

    @pl.when(tiles > 0)
    def _():
        s_now[...] = score(0)

    def step(t, _):
        s_next[...] = score(t + 1)
        update(t, s_now[...])
        s_now[...] = s_next[...]
        return 0

    lax.fori_loop(0, tiles - 1, step, 0)

    @pl.when(tiles > 0)
    def _():
        update(tiles - 1, s_now[...])

    if last:
        av_copy.wait()
        for half in range(2):
            for h in range(HD):
                cols = slice(h * HALF, (h + 1) * HALF)
                lat = (acc[half, :, cols] / l_ref[half, :, cols]).astype(jnp.bfloat16)
                out_ref[half * HALF : (half + 1) * HALF, cols] = lax.dot_general(
                    lat, av_ref[h], (((0,), (0,)), ((), ())), preferred_element_type=jnp.float32
                ).astype(jnp.bfloat16)


VM = pl.BlockSpec(memory_space=pltpu.VMEM)
SM = pl.BlockSpec(memory_space=pltpu.SMEM)
FREE = pl.BlockSpec(memory_space=pl.ANY)


def after(x, token):
    return pl.pallas_call(
        gate_kernel,
        out_shape=jax.ShapeDtypeStruct(x.shape, x.dtype),
        in_specs=[FREE, FREE],
        out_specs=FREE,
        input_output_aliases={0: 0},
        compiler_params=pltpu.CompilerParams(vmem_limit_bytes=2**20),
        cost_estimate=pl.CostEstimate(flops=1000, bytes_accessed=1000, transcendentals=0),
    )(x, token)


def attend(place, block_owner, queries, pieces, slots, state=None, value=None):
    first, last = state is None, value is not None
    n = 4 * len(pieces)
    state_shapes = ((2, LATENT, 512), (2, 1, 512), (2, 1, 512))
    scratch = [pltpu.VMEM((n, KV, HALF), jnp.bfloat16)]
    aliases = {}
    if last and first:
        scratch += [pltpu.VMEM(s, jnp.float32) for s in state_shapes]
    if last:
        out = jax.ShapeDtypeStruct((256, 512), jnp.bfloat16)
    else:
        out = [jax.ShapeDtypeStruct(s, jnp.float32) for s in state_shapes]
    scratch += [pltpu.VMEM((512, 512), jnp.float32)] * 2
    scratch += [pltpu.SMEM((NB,), jnp.int32), pltpu.SMEM((NB + 1,), jnp.int32)]
    if last:
        scratch += [pltpu.VMEM((HD, LATENT, 128), jnp.bfloat16), pltpu.SemaphoreType.DMA]
    specs = [SM, SM, VM] + ([FREE] if last else [])
    args = [place, block_owner, queries]
    args += [value] if last else []
    if not (first or last):
        aliases = {len(args) + i: i for i in range(3)}
    args += [] if first else list(state)
    args += pieces
    return pl.pallas_call(
        functools.partial(attend_kernel, slots, first, last),
        out_shape=out,
        in_specs=specs + [VM] * (len(args) - len(specs)),
        out_specs=VM if last else [VM] * 3,
        scratch_shapes=scratch,
        input_output_aliases=aliases,
        compiler_params=pltpu.CompilerParams(vmem_limit_bytes=16 * 2**20),
        cost_estimate=pl.CostEstimate(
            flops=n * 1_000_000, bytes_accessed=n * 1_000, transcendentals=0
        ),
    )(*args)


def per_device(query_latent, norm_gain, kv_latent, q_up, absorb_key, absorb_value, block_owner):
    ctx, head = lax.axis_index("ctx"), lax.axis_index("head")
    me_x, me_y, me_c = (ctx // 2) % 4, (ctx // 8) * 2 + head // 8, ctx % 2
    place = jnp.stack([me_x, me_y, me_c]).astype(jnp.int32)

    z_groups = [list(range(8)), list(range(8, 16))]
    q_spread = pl.pallas_call(
        spread_kernel,
        out_shape=jax.ShapeDtypeStruct((8, 32, QLAT), jnp.bfloat16),
        in_specs=[VM] * 2,
        out_specs=VM,
        compiler_params=pltpu.CompilerParams(vmem_limit_bytes=4 * 2**20),
    )(query_latent, move(query_latent, swap_row))

    own = lax.all_to_all(
        jnp.broadcast_to(kv_latent[None], (8,) + kv_latent.shape),
        "head", 0, 0, axis_index_groups=z_groups, tiled=True
    ).reshape(HALF, KV)

    rows = lax.all_to_all(q_spread, "head", 0, 0, axis_index_groups=z_groups, tiled=True)

    blocks = [own] + [move(own, shift(k, True)) for k in SHIFTS]
    stack = pl.pallas_call(
        turn_kernel,
        out_shape=jax.ShapeDtypeStruct((4, KV, HALF), jnp.bfloat16),
        in_specs=[VM] * 4,
        out_specs=VM,
        compiler_params=pltpu.CompilerParams(vmem_limit_bytes=8 * 2**20),
    )(*blocks)
    near = {0: stack}
    for k in SHIFTS:
        near[k] = move(stack, shift(k, False))
    p = block_owner[ctx]
    offset = jnp.arange(256, dtype=jnp.int32)
    in_low = (offset < HALF) == (me_y % 2 == 0)
    pos = jnp.where(in_low, p, NB - 1 - p) * HALF + (offset & (HALF - 1))
    freq = jnp.exp(jnp.arange(ROPE // 2, dtype=jnp.float32) * (-math.log(10000.0) / (ROPE // 2)))
    angles = freq[:, None] * pos.astype(jnp.float32)
    queries = pl.pallas_call(
        project_kernel,
        out_shape=jax.ShapeDtypeStruct((2, KV, 512), jnp.bfloat16),
        in_specs=[SM] + [VM] * 4 + [FREE] * 2,
        out_specs=VM,
        scratch_shapes=[
            pltpu.VMEM(q_up.shape, jnp.bfloat16),
            pltpu.VMEM(absorb_key.shape, jnp.bfloat16),
            pltpu.SemaphoreType.DMA((12,)),
        ],
        compiler_params=pltpu.CompilerParams(vmem_limit_bytes=50 * 2**20),
        cost_estimate=pl.CostEstimate(flops=750_000_000, bytes_accessed=5_000_000, transcendentals=0),
    )(place, rows, norm_gain.reshape(1, QLAT), jnp.cos(angles), jnp.sin(angles), q_up, absorb_key)

    distant = {0: move(stack, swap_core)}

    def part(keys, **more):
        pieces = [near[k] for k in keys] + [distant[k] for k in keys]
        kinds = tuple((far, k) for far in range(2) for k in keys)
        return attend(place, block_owner, queries, pieces, kinds, **more)

    state = part([0])
    for k in SHIFTS:
        near[k] = after(near[k], state[1])
        distant[k] = move(near[k], swap_core)
    return part([1, 3, 2], state=state, value=absorb_value)


def solution(mesh):
    return jax.shard_map(
        per_device,
        mesh=mesh,
        in_specs=(
            P(AXES, None),
            P(),
            P(AXES, None),
            P(None, "head"),
            P("head", None, None),
            P("head", None, None),
            P(),
        ),
        out_specs=P("ctx", "head"),
        check_vma=False,
    )
```

```python
import functools
import math

import jax
import jax.numpy as jnp
from jax import lax
from jax.experimental import pallas as pl
from jax.experimental.pallas import tpu as pltpu
from jax.sharding import PartitionSpec as P

QLAT = 1536
LATENT = 512
ROPE = 64
NOPE = 128
KV = LATENT + ROPE
HD = 4
HALF = 128
NB = 32
EPS = 1e-06
SCALE2 = float(NOPE + ROPE) ** (-0.5) * math.log2(math.e)
MASKED = -1e30
AXES = ("ctx", "head")
SHIFTS = (2, 3, 1)


def flat(x, y, z, c):
    x, y, z, c = x % 4, y % 4, z % 8, c % 2
    return (((y // 2) * 4 + x) * 2 + c) * 16 + (y % 2) * 8 + z


def move(a, to):
    pairs = []
    for x in range(4):
        for y in range(4):
            for z in range(8):
                for c in range(2):
                    pairs.append((flat(x, y, z, c), flat(*to(x, y, z, c))))
    return lax.ppermute(a, AXES, pairs)


def shift(k, first):
    def to(x, y, z, c):
        return (x + k, y, z, c) if (c == 0) == first else (x, y + k, z, c)

    return to


def swap_row(x, y, z, c):
    return (x, y ^ 1, z, c)


def swap_core(x, y, z, c):
    return (x, y, z, c + 1)


def spread_kernel(q_ref, pair_ref, q_out):
    both = jnp.concatenate([q_ref[...], pair_ref[...]], axis=0)
    q_out[...] = jnp.broadcast_to(both[None], q_out.shape)


def turn_kernel(*refs):
    for i in range(4):
        refs[4][i] = refs[i][...].T


def gate_kernel(_x, _token, _out):
    pass


def project_kernel(place_ref, q_ref, gain_ref, cos_ref, sin_ref, up_ref, ak_ref, out_ref):
    own = place_ref[1] & 1
    gain = gain_ref[...].astype(jnp.float32)
    halves = []
    for k in range(2):
        x = q_ref[:, 16 * k : 16 * k + 16].reshape(HALF, QLAT).astype(jnp.float32)
        ms = jnp.mean(x * x, axis=-1, keepdims=True)
        halves.append((x * lax.rsqrt(ms + EPS) * gain).astype(jnp.bfloat16))
    normed = jnp.concatenate(halves, axis=0)
    proj = lax.dot_general(
        up_ref[...], normed, (((0,), (1,)), ((), ())), preferred_element_type=jnp.float32
    )
    cos, sin = cos_ref[...], sin_ref[...]
    for h in range(HD):
        base = h * (NOPE + ROPE)
        nope = proj[base : base + NOPE].astype(jnp.bfloat16)
        a = proj[base + NOPE : base + NOPE + ROPE // 2]
        b = proj[base + NOPE + ROPE // 2 : base + NOPE + ROPE]
        pe = jnp.concatenate([a * cos - b * sin, a * sin + b * cos], axis=0).astype(jnp.bfloat16)
        qa = lax.dot_general(
            ak_ref[h], nope, (((0,), (0,)), ((), ())), preferred_element_type=jnp.float32
        ).astype(jnp.bfloat16)
        for k in range(2):
            half = own if k == 0 else 1 - own
            cols = slice(h * HALF, (h + 1) * HALF)
            out_ref[half, :LATENT, cols] = qa[:, k * HALF : (k + 1) * HALF]
            out_ref[half, LATENT:, cols] = pe[:, k * HALF : (k + 1) * HALF]


def attend_kernel(slots, first, last, place_ref, owner_ref, q_ref, *rest):
    rest = list(rest)
    if last:
        av_src = rest.pop(0)
    if not first:
        state = [rest.pop(0) for _ in range(3)]
    pieces = [rest.pop(0) for _ in slots]
    if last:
        out_ref = rest.pop(0)
    else:
        state = [rest.pop(0) for _ in range(3)]
    keys = rest.pop(0)
    if first and last:
        state = [rest.pop(0) for _ in range(3)]
    acc, m_ref, l_ref = state
    s_now, s_next, rank, bpos = rest[:4]
    if last:
        av_ref, av_sem = rest[4:]
        av_copy = pltpu.make_async_copy(av_src, av_ref, av_sem)
        av_copy.start()
    me_x, me_y, me_c = place_ref[0], place_ref[1], place_ref[2]

    where = []
    for b in range(NB):
        rank[b] = 0
    along = (0,) + SHIFTS
    for far, second in slots:
        core = me_c if far == 0 else 1 - me_c
        for i in range(4):
            dx = jnp.where(core == 0, along[i], second)
            dy = jnp.where(core == 0, second, along[i])
            x = (me_x - dx + 4) & 3
            y = (me_y - dy + 4) & 3
            p = owner_ref[(y >> 1) * 8 + x * 2 + core]
            b = jnp.where((y & 1) == 0, p, NB - 1 - p)
            rank[b] = 1
            where.append(b)
    mine = owner_ref[(me_y >> 1) * 8 + me_x * 2 + me_c]
    other = NB - 1 - mine
    count = jnp.int32(0)
    low = jnp.int32(0)
    high = jnp.int32(0)
    for b in range(NB):
        here = rank[b]
        rank[b] = count
        bpos[count] = b
        count = count + here
        low = low + jnp.where(b <= mine, here, 0)
        high = high + jnp.where(b <= other, here, 0)
    for s, b in enumerate(where):
        keys[rank[b]] = pieces[s // 4][s % 4]

    if first:
        acc[...] = jnp.zeros_like(acc)
        m_ref[...] = jnp.full_like(m_ref, MASKED)
        l_ref[...] = jnp.zeros_like(l_ref)

    tiles_high = (high + 3) // 4
    tiles = tiles_high + (low + 3) // 4
    delta = (
        lax.broadcasted_iota(jnp.int32, (HALF, 512), 0)
        - (lax.broadcasted_iota(jnp.int32, (HALF, 512), 1) & (HALF - 1))
    )

    def at(t):
        is_high = t < tiles_high
        half = jnp.where(is_high, 1, 0)
        return half, jnp.where(is_high, t, t - tiles_high), jnp.where(is_high, other, mine)

    def load(j):
        return jnp.concatenate([keys[4 * j + i] for i in range(4)], axis=1)

    def score(t):
        half, j, a = at(t)
        s = lax.dot_general(
            load(j), q_ref[half], (((0,), (0,)), ((), ())), preferred_element_type=jnp.float32
        )
        return jnp.concatenate(
            [
                jnp.where(
                    delta <= (a - bpos[4 * j + i]) * HALF, s[i * HALF : (i + 1) * HALF], MASKED
                )
                for i in range(4)
            ],
            axis=0,
        )

    def update(t, s):
        half, j, _ = at(t)
        old = m_ref[half]
        new = jnp.maximum(old, jnp.max(s, axis=0, keepdims=True))
        w = jnp.exp2((s - new) * SCALE2)
        f = jnp.exp2((old - new) * SCALE2)
        m_ref[half] = new
        l_ref[half] = l_ref[half] * f + jnp.sum(w, axis=0, keepdims=True)
        acc[half] = acc[half] * f + jnp.dot(
            load(j)[:LATENT], w.astype(jnp.bfloat16), preferred_element_type=jnp.float32
        )

    @pl.when(tiles > 0)
    def _():
        s_now[...] = score(0)

    def step(t, _):
        s_next[...] = score(t + 1)
        update(t, s_now[...])
        s_now[...] = s_next[...]
        return 0

    lax.fori_loop(0, tiles - 1, step, 0)

    @pl.when(tiles > 0)
    def _():
        update(tiles - 1, s_now[...])

    if last:
        av_copy.wait()
        for half in range(2):
            for h in range(HD):
                cols = slice(h * HALF, (h + 1) * HALF)
                lat = (acc[half, :, cols] * (1.0 / l_ref[half, :, cols])).astype(jnp.bfloat16)
                out_ref[half * HALF : (half + 1) * HALF, cols] = lax.dot_general(
                    lat, av_ref[h], (((0,), (0,)), ((), ())), preferred_element_type=jnp.float32
                ).astype(jnp.bfloat16)


VM = pl.BlockSpec(memory_space=pltpu.VMEM)
SM = pl.BlockSpec(memory_space=pltpu.SMEM)
FREE = pl.BlockSpec(memory_space=pl.ANY)


def after(x, token):
    return pl.pallas_call(
        gate_kernel,
        out_shape=jax.ShapeDtypeStruct(x.shape, x.dtype),
        in_specs=[FREE, FREE],
        out_specs=FREE,
        input_output_aliases={0: 0},
        compiler_params=pltpu.CompilerParams(vmem_limit_bytes=2**20),
        cost_estimate=pl.CostEstimate(flops=1000, bytes_accessed=1000, transcendentals=0),
    )(x, token)


def attend(place, block_owner, queries, pieces, slots, state=None, value=None):
    first, last = state is None, value is not None
    n = 4 * len(pieces)
    state_shapes = ((2, LATENT, 512), (2, 1, 512), (2, 1, 512))
    scratch = [pltpu.VMEM((n, KV, HALF), jnp.bfloat16)]
    aliases = {}
    if last and first:
        scratch += [pltpu.VMEM(s, jnp.float32) for s in state_shapes]
    if last:
        out = jax.ShapeDtypeStruct((256, 512), jnp.bfloat16)
    else:
        out = [jax.ShapeDtypeStruct(s, jnp.float32) for s in state_shapes]
    scratch += [pltpu.VMEM((512, 512), jnp.float32)] * 2
    scratch += [pltpu.SMEM((NB,), jnp.int32), pltpu.SMEM((NB + 1,), jnp.int32)]
    if last:
        scratch += [pltpu.VMEM((HD, LATENT, 128), jnp.bfloat16), pltpu.SemaphoreType.DMA]
    specs = [SM, SM, VM] + ([FREE] if last else [])
    args = [place, block_owner, queries]
    args += [value] if last else []
    if not (first or last):
        aliases = {len(args) + i: i for i in range(3)}
    args += [] if first else list(state)
    args += pieces
    return pl.pallas_call(
        functools.partial(attend_kernel, slots, first, last),
        out_shape=out,
        in_specs=specs + [VM] * (len(args) - len(specs)),
        out_specs=VM if last else [VM] * 3,
        scratch_shapes=scratch,
        input_output_aliases=aliases,
        compiler_params=pltpu.CompilerParams(vmem_limit_bytes=16 * 2**20),
        cost_estimate=pl.CostEstimate(
            flops=n * 1_000_000, bytes_accessed=n * 1_000, transcendentals=0
        ),
    )(*args)


def per_device(query_latent, norm_gain, kv_latent, q_up, absorb_key, absorb_value, block_owner):
    ctx, head = lax.axis_index("ctx"), lax.axis_index("head")
    me_x, me_y, me_c = (ctx // 2) % 4, (ctx // 8) * 2 + head // 8, ctx % 2
    place = jnp.stack([me_x, me_y, me_c]).astype(jnp.int32)

    z_groups = [list(range(8)), list(range(8, 16))]
    q_spread = pl.pallas_call(
        spread_kernel,
        out_shape=jax.ShapeDtypeStruct((8, 32, QLAT), jnp.bfloat16),
        in_specs=[VM] * 2,
        out_specs=VM,
        compiler_params=pltpu.CompilerParams(vmem_limit_bytes=4 * 2**20),
    )(query_latent, move(query_latent, swap_row))

    own = lax.all_to_all(
        jnp.broadcast_to(kv_latent[None], (8,) + kv_latent.shape),
        "head", 0, 0, axis_index_groups=z_groups, tiled=True
    ).reshape(HALF, KV)

    rows = lax.all_to_all(q_spread, "head", 0, 0, axis_index_groups=z_groups, tiled=True)

    blocks = [own] + [move(own, shift(k, True)) for k in SHIFTS]
    stack = pl.pallas_call(
        turn_kernel,
        out_shape=jax.ShapeDtypeStruct((4, KV, HALF), jnp.bfloat16),
        in_specs=[VM] * 4,
        out_specs=VM,
        compiler_params=pltpu.CompilerParams(vmem_limit_bytes=8 * 2**20),
    )(*blocks)
    near = {0: stack}
    for k in SHIFTS:
        near[k] = move(stack, shift(k, False))
    p = block_owner[ctx]
    offset = jnp.arange(256, dtype=jnp.int32)
    in_low = (offset < HALF) == (me_y % 2 == 0)
    pos = jnp.where(in_low, p, NB - 1 - p) * HALF + (offset & (HALF - 1))
    freq = jnp.exp(jnp.arange(ROPE // 2, dtype=jnp.float32) * (-math.log(10000.0) / (ROPE // 2)))
    angles = freq[:, None] * pos.astype(jnp.float32)
    queries = pl.pallas_call(
        project_kernel,
        out_shape=jax.ShapeDtypeStruct((2, KV, 512), jnp.bfloat16),
        in_specs=[SM] + [VM] * 6,
        out_specs=VM,
        compiler_params=pltpu.CompilerParams(vmem_limit_bytes=16 * 2**20),
        cost_estimate=pl.CostEstimate(flops=750_000_000, bytes_accessed=5_000_000, transcendentals=0),
    )(place, rows, norm_gain.reshape(1, QLAT), jnp.cos(angles), jnp.sin(angles), q_up, absorb_key)

    distant = {0: move(stack, swap_core)}

    def part(keys, **more):
        pieces = [near[k] for k in keys] + [distant[k] for k in keys]
        kinds = tuple((far, k) for far in range(2) for k in keys)
        return attend(place, block_owner, queries, pieces, kinds, **more)

    state = part([0])
    for k in SHIFTS:
        near[k] = after(near[k], state[1])
        distant[k] = move(near[k], swap_core)
    return part([1, 3, 2], state=state, value=absorb_value)


def solution(mesh):
    return jax.shard_map(
        per_device,
        mesh=mesh,
        in_specs=(
            P(AXES, None),
            P(),
            P(AXES, None),
            P(None, "head"),
            P("head", None, None),
            P("head", None, None),
            P(),
        ),
        out_specs=P("ctx", "head"),
        check_vma=False,
    )
```

```python
import functools
import math

import jax
import jax.numpy as jnp
from jax import lax
from jax.experimental import pallas as pl
from jax.experimental.pallas import tpu as pltpu
from jax.sharding import PartitionSpec as P

QLAT = 1536
LATENT = 512
ROPE = 64
NOPE = 128
KV = LATENT + ROPE
HD = 4
HALF = 128
NB = 32
EPS = 1e-06
SCALE2 = float(NOPE + ROPE) ** (-0.5) * math.log2(math.e)
MASKED = -1e30
AXES = ("ctx", "head")
SHIFTS = (2, 3, 1)


def flat(x, y, z, c):
    x, y, z, c = x % 4, y % 4, z % 8, c % 2
    return (((y // 2) * 4 + x) * 2 + c) * 16 + (y % 2) * 8 + z


def move(a, to):
    pairs = []
    for x in range(4):
        for y in range(4):
            for z in range(8):
                for c in range(2):
                    pairs.append((flat(x, y, z, c), flat(*to(x, y, z, c))))
    return lax.ppermute(a, AXES, pairs)


def shift(k, first):
    def to(x, y, z, c):
        return (x + k, y, z, c) if (c == 0) == first else (x, y + k, z, c)

    return to


def swap_row(x, y, z, c):
    return (x, y ^ 1, z, c)


def swap_core(x, y, z, c):
    return (x, y, z, c + 1)


def spread_kernel(q_ref, pair_ref, q_out):
    both = jnp.concatenate([q_ref[...], pair_ref[...]], axis=0)
    q_out[...] = jnp.broadcast_to(both[None], q_out.shape)


def turn_kernel(*refs):
    for i in range(4):
        refs[4][i] = refs[i][...].T


def gate_kernel(_x, _token, _out):
    pass


def project_kernel(place_ref, q_ref, gain_ref, cos_ref, sin_ref, up_ref, ak_ref, out_ref):
    own = place_ref[1] & 1
    x = jnp.concatenate(
        [q_ref[:, 16 * k : 16 * k + 16].reshape(HALF, QLAT) for k in range(2)], axis=0
    ).astype(jnp.float32)
    ms = jnp.mean(x * x, axis=-1, keepdims=True)
    normed = (x * lax.rsqrt(ms + EPS) * gain_ref[...].astype(jnp.float32)).astype(jnp.bfloat16)
    proj = lax.dot_general(
        up_ref[...], normed, (((0,), (1,)), ((), ())), preferred_element_type=jnp.float32
    )
    cos, sin = cos_ref[...], sin_ref[...]
    for h in range(HD):
        base = h * (NOPE + ROPE)
        nope = proj[base : base + NOPE].astype(jnp.bfloat16)
        a = proj[base + NOPE : base + NOPE + ROPE // 2]
        b = proj[base + NOPE + ROPE // 2 : base + NOPE + ROPE]
        pe = jnp.concatenate([a * cos - b * sin, a * sin + b * cos], axis=0).astype(jnp.bfloat16)
        qa = lax.dot_general(
            ak_ref[h], nope, (((0,), (0,)), ((), ())), preferred_element_type=jnp.float32
        ).astype(jnp.bfloat16)
        for k in range(2):
            half = own if k == 0 else 1 - own
            cols = slice(h * HALF, (h + 1) * HALF)
            out_ref[half, :LATENT, cols] = qa[:, k * HALF : (k + 1) * HALF]
            out_ref[half, LATENT:, cols] = pe[:, k * HALF : (k + 1) * HALF]


def attend_kernel(slots, first, last, place_ref, owner_ref, q_ref, *rest):
    rest = list(rest)
    if last:
        av_src = rest.pop(0)
    if not first:
        state = [rest.pop(0) for _ in range(3)]
    pieces = [rest.pop(0) for _ in slots]
    if last:
        out_ref = rest.pop(0)
    else:
        state = [rest.pop(0) for _ in range(3)]
    keys = rest.pop(0)
    if first and last:
        state = [rest.pop(0) for _ in range(3)]
    acc, m_ref, l_ref = state
    s_now, s_next, rank, bpos = rest[:4]
    if last:
        av_ref, av_sem = rest[4:]
        av_copy = pltpu.make_async_copy(av_src, av_ref, av_sem)
        av_copy.start()
    me_x, me_y, me_c = place_ref[0], place_ref[1], place_ref[2]

    where = []
    for b in range(NB):
        rank[b] = 0
    along = (0,) + SHIFTS
    for far, second in slots:
        core = me_c if far == 0 else 1 - me_c
        for i in range(4):
            dx = jnp.where(core == 0, along[i], second)
            dy = jnp.where(core == 0, second, along[i])
            x = (me_x - dx + 4) & 3
            y = (me_y - dy + 4) & 3
            p = owner_ref[(y >> 1) * 8 + x * 2 + core]
            b = jnp.where((y & 1) == 0, p, NB - 1 - p)
            rank[b] = 1
            where.append(b)
    mine = owner_ref[(me_y >> 1) * 8 + me_x * 2 + me_c]
    other = NB - 1 - mine
    count = jnp.int32(0)
    low = jnp.int32(0)
    high = jnp.int32(0)
    for b in range(NB):
        here = rank[b]
        rank[b] = count
        bpos[count] = b
        count = count + here
        low = low + jnp.where(b <= mine, here, 0)
        high = high + jnp.where(b <= other, here, 0)
    for s, b in enumerate(where):
        keys[rank[b]] = pieces[s // 4][s % 4]

    if first:
        acc[...] = jnp.zeros_like(acc)
        m_ref[...] = jnp.full_like(m_ref, MASKED)
        l_ref[...] = jnp.zeros_like(l_ref)

    tiles_high = (high + 3) // 4
    tiles = tiles_high + (low + 3) // 4
    delta = (
        lax.broadcasted_iota(jnp.int32, (HALF, 512), 0)
        - (lax.broadcasted_iota(jnp.int32, (HALF, 512), 1) & (HALF - 1))
    )

    def at(t):
        is_high = t < tiles_high
        half = jnp.where(is_high, 1, 0)
        return half, jnp.where(is_high, t, t - tiles_high), jnp.where(is_high, other, mine)

    def load(j):
        return jnp.concatenate([keys[4 * j + i] for i in range(4)], axis=1)

    def score(t):
        half, j, a = at(t)
        s = lax.dot_general(
            load(j), q_ref[half], (((0,), (0,)), ((), ())), preferred_element_type=jnp.float32
        )
        return jnp.concatenate(
            [
                jnp.where(
                    delta <= (a - bpos[4 * j + i]) * HALF, s[i * HALF : (i + 1) * HALF], MASKED
                )
                for i in range(4)
            ],
            axis=0,
        )

    def update(t, s):
        half, j, _ = at(t)
        old = m_ref[half]
        new = jnp.maximum(old, jnp.max(s, axis=0, keepdims=True))
        w = jnp.exp2((s - new) * SCALE2)
        f = jnp.exp2((old - new) * SCALE2)
        m_ref[half] = new
        l_ref[half] = l_ref[half] * f + jnp.sum(w, axis=0, keepdims=True)
        acc[half] = acc[half] * f + jnp.dot(
            load(j)[:LATENT], w.astype(jnp.bfloat16), preferred_element_type=jnp.float32
        )

    @pl.when(tiles > 0)
    def _():
        s_now[...] = score(0)

    def step(t, _):
        s_next[...] = score(t + 1)
        update(t, s_now[...])
        s_now[...] = s_next[...]
        return 0

    lax.fori_loop(0, tiles - 1, step, 0)

    @pl.when(tiles > 0)
    def _():
        update(tiles - 1, s_now[...])

    if last:
        av_copy.wait()
        for half in range(2):
            for h in range(HD):
                cols = slice(h * HALF, (h + 1) * HALF)
                lat = (acc[half, :, cols] / l_ref[half, :, cols]).astype(jnp.bfloat16)
                out_ref[half * HALF : (half + 1) * HALF, cols] = lax.dot_general(
                    lat, av_ref[h], (((0,), (0,)), ((), ())), preferred_element_type=jnp.float32
                ).astype(jnp.bfloat16)


VM = pl.BlockSpec(memory_space=pltpu.VMEM)
SM = pl.BlockSpec(memory_space=pltpu.SMEM)
FREE = pl.BlockSpec(memory_space=pl.ANY)


def after(x, token):
    return pl.pallas_call(
        gate_kernel,
        out_shape=jax.ShapeDtypeStruct(x.shape, x.dtype),
        in_specs=[FREE, FREE],
        out_specs=FREE,
        input_output_aliases={0: 0},
        compiler_params=pltpu.CompilerParams(vmem_limit_bytes=2**20),
        cost_estimate=pl.CostEstimate(flops=1000, bytes_accessed=1000, transcendentals=0),
    )(x, token)


def attend(place, block_owner, queries, pieces, slots, state=None, value=None):
    first, last = state is None, value is not None
    n = 4 * len(pieces)
    state_shapes = ((2, LATENT, 512), (2, 1, 512), (2, 1, 512))
    scratch = [pltpu.VMEM((n, KV, HALF), jnp.bfloat16)]
    aliases = {}
    if last and first:
        scratch += [pltpu.VMEM(s, jnp.float32) for s in state_shapes]
    if last:
        out = jax.ShapeDtypeStruct((256, 512), jnp.bfloat16)
    else:
        out = [jax.ShapeDtypeStruct(s, jnp.float32) for s in state_shapes]
    scratch += [pltpu.VMEM((512, 512), jnp.float32)] * 2
    scratch += [pltpu.SMEM((NB,), jnp.int32), pltpu.SMEM((NB + 1,), jnp.int32)]
    if last:
        scratch += [pltpu.VMEM((HD, LATENT, 128), jnp.bfloat16), pltpu.SemaphoreType.DMA]
    specs = [SM, SM, VM] + ([FREE] if last else [])
    args = [place, block_owner, queries]
    args += [value] if last else []
    if not (first or last):
        aliases = {len(args) + i: i for i in range(3)}
    args += [] if first else list(state)
    args += pieces
    return pl.pallas_call(
        functools.partial(attend_kernel, slots, first, last),
        out_shape=out,
        in_specs=specs + [VM] * (len(args) - len(specs)),
        out_specs=VM if last else [VM] * 3,
        scratch_shapes=scratch,
        input_output_aliases=aliases,
        compiler_params=pltpu.CompilerParams(vmem_limit_bytes=11 * 2**20),
        cost_estimate=pl.CostEstimate(
            flops=n * 1_000_000, bytes_accessed=n * 1_000, transcendentals=0
        ),
    )(*args)


def per_device(query_latent, norm_gain, kv_latent, q_up, absorb_key, absorb_value, block_owner):
    ctx, head = lax.axis_index("ctx"), lax.axis_index("head")
    me_x, me_y, me_c = (ctx // 2) % 4, (ctx // 8) * 2 + head // 8, ctx % 2
    place = jnp.stack([me_x, me_y, me_c]).astype(jnp.int32)

    z_groups = [list(range(8)), list(range(8, 16))]
    q_spread = pl.pallas_call(
        spread_kernel,
        out_shape=jax.ShapeDtypeStruct((8, 32, QLAT), jnp.bfloat16),
        in_specs=[VM] * 2,
        out_specs=VM,
        compiler_params=pltpu.CompilerParams(vmem_limit_bytes=4 * 2**20),
    )(query_latent, move(query_latent, swap_row))

    own = lax.all_to_all(
        jnp.broadcast_to(kv_latent[None], (8,) + kv_latent.shape),
        "head", 0, 0, axis_index_groups=z_groups, tiled=True
    ).reshape(HALF, KV)

    rows = lax.all_to_all(q_spread, "head", 0, 0, axis_index_groups=z_groups, tiled=True)

    blocks = [own] + [move(own, shift(k, True)) for k in SHIFTS]
    stack = pl.pallas_call(
        turn_kernel,
        out_shape=jax.ShapeDtypeStruct((4, KV, HALF), jnp.bfloat16),
        in_specs=[VM] * 4,
        out_specs=VM,
        compiler_params=pltpu.CompilerParams(vmem_limit_bytes=8 * 2**20),
    )(*blocks)
    near = {0: stack}
    for k in SHIFTS:
        near[k] = move(stack, shift(k, False))
    p = block_owner[ctx]
    offset = jnp.arange(256, dtype=jnp.int32)
    in_low = (offset < HALF) == (me_y % 2 == 0)
    pos = jnp.where(in_low, p, NB - 1 - p) * HALF + (offset & (HALF - 1))
    freq = jnp.exp(jnp.arange(ROPE // 2, dtype=jnp.float32) * (-math.log(10000.0) / (ROPE // 2)))
    angles = freq[:, None] * pos.astype(jnp.float32)
    queries = pl.pallas_call(
        project_kernel,
        out_shape=jax.ShapeDtypeStruct((2, KV, 512), jnp.bfloat16),
        in_specs=[SM] + [VM] * 6,
        out_specs=VM,
        compiler_params=pltpu.CompilerParams(vmem_limit_bytes=11 * 2**20),
        cost_estimate=pl.CostEstimate(flops=750_000_000, bytes_accessed=5_000_000, transcendentals=0),
    )(place, rows, norm_gain.reshape(1, QLAT), jnp.cos(angles), jnp.sin(angles), q_up, absorb_key)

    distant = {0: move(stack, swap_core)}

    def part(keys, **more):
        pieces = [near[k] for k in keys] + [distant[k] for k in keys]
        kinds = tuple((far, k) for far in range(2) for k in keys)
        return attend(place, block_owner, queries, pieces, kinds, **more)

    state = part([0])
    for k in SHIFTS:
        near[k] = after(near[k], state[1])
        distant[k] = move(near[k], swap_core)
    return part([1, 3, 2], state=state, value=absorb_value)


def solution(mesh):
    return jax.shard_map(
        per_device,
        mesh=mesh,
        in_specs=(
            P(AXES, None),
            P(),
            P(AXES, None),
            P(None, "head"),
            P("head", None, None),
            P("head", None, None),
            P(),
        ),
        out_specs=P("ctx", "head"),
        check_vma=False,
    )
```
